512 devices in a mesh: batch: 128 (over x_hi, y, z), mp: 4 (over x_lo, core).
Axes of the slice: x: 4 (x_hi: 2, x_lo: 2; x = x_hi * 2 + x_lo), y: 8, z: 8, core: 2. Of those that a mesh axis runs over, the one named last changes fastest.
Arguments:
- queries: bfloat16 [1024, 4096], P('batch', 'mp')
- paraphrases: bfloat16 [1024, 4096], P('batch', 'mp')
- partner: int32 [1024], P('batch'), may hold values from 0 to 1023, as said below
- logit_scale: float32 [], replicated
Outputs:
- loss: float32 [], replicated
- grad_queries: bfloat16 [1024, 4096], P('batch', 'mp')
- grad_paraphrases: bfloat16 [1024, 4096], P('batch', 'mp')
The draws below stay inside these ranges and needn't reach their ends.
Inputs may be any that keep to these rules, and one draw needn't show every extreme that they name: partner is a permutation of the 1024 paraphrase rows.
All inputs are finite; a program needn't handle non-finite values.
Results may differ from the reference program's by a relative error of at most 0.006.
Values may be sent and summed in bfloat16 or wider, within the bound.
A program may use at most 64 MiB of HBM per device.

```python
import jax
import jax.numpy as jnp
from jax import lax

D = 4096
PAIRS = 1024


def pair_order(key):
    return jax.random.permutation(jax.random.fold_in(key, 101), PAIRS).astype(jnp.int32)


def base_rows(key, spread):
    first, second = jax.random.split(jax.random.fold_in(key, 202), 2)
    noise = jax.random.normal(first, (PAIRS, D), jnp.float32)
    scales = jnp.exp(spread * jax.random.uniform(second, (PAIRS, 1), jnp.float32))
    return (noise, scales)


def draw_queries(key, part):
    rows, scales = base_rows(key, 2.3)
    return (rows * scales).astype(jnp.bfloat16)


def draw_paraphrases(key, part):
    order = pair_order(key)
    rows, scales = base_rows(key, 2.3)
    low, high = (0.1, 0.6)
    key = jax.random.fold_in(key, 3)
    first, second, third = jax.random.split(key, 3)
    strength = jax.random.uniform(first, (PAIRS, 1), jnp.float32, low, high)
    fresh = jax.random.normal(second, (PAIRS, D), jnp.float32)
    own_scale = jnp.exp(2.3 * jax.random.uniform(third, (PAIRS, 1), jnp.float32))
    inverse = jnp.argsort(order, stable=True)
    paired = (strength * rows)[inverse]
    return ((paired + fresh) * own_scale).astype(jnp.bfloat16)


def draw_partner(key, part):
    return pair_order(key)


def draw_logit_scale(key, part):
    key = jax.random.fold_in(key, 5)
    return jax.random.uniform(key, (), jnp.float32, 8.0, 20.0)


def setup_inputs(seed: int = 0) -> dict:
    arg_keys = jax.random.split(jax.random.key(seed), 5)
    return {
        "queries": draw_queries(jax.random.fold_in(arg_keys[4], 71), 0),
        "paraphrases": draw_paraphrases(jax.random.fold_in(arg_keys[4], 71), 0),
        "partner": draw_partner(jax.random.fold_in(arg_keys[4], 71), 0),
        "logit_scale": draw_logit_scale(jax.random.fold_in(arg_keys[4], 71), 0),
    }


def unit_rows(values):
    whole = values.astype(jnp.float32)
    norm = jnp.sqrt(lax.optimization_barrier(jnp.sum(whole * whole, axis=1)) + 1e-06)
    return (whole / norm[:, None], norm)

def reference(queries, paraphrases, partner, logit_scale):
    q_unit, q_norm = unit_rows(queries)
    p_unit, p_norm = unit_rows(paraphrases)
    q_half = q_unit.astype(jnp.bfloat16)
    p_half = p_unit.astype(jnp.bfloat16)
    scores = logit_scale * jnp.dot(q_half, p_half.T, preferred_element_type=jnp.float32)
    row_max = lax.optimization_barrier(jnp.max(scores, axis=1))
    row_lse = row_max + jnp.log(lax.optimization_barrier(jnp.sum(jnp.exp(scores - row_max[:, None]), axis=1)))
    col_max = lax.optimization_barrier(jnp.max(scores, axis=0))
    col_lse = col_max + jnp.log(lax.optimization_barrier(jnp.sum(jnp.exp(scores - col_max[None, :]), axis=0)))
    columns = jnp.arange(PAIRS, dtype=jnp.int32)
    hit = (partner[:, None] == columns[None, :]).astype(jnp.float32)
    positive = lax.optimization_barrier(jnp.sum(hit * scores, axis=1))
    loss = 0.5 * jnp.mean(row_lse) + 0.5 * jnp.mean(col_lse) - jnp.mean(positive)
    weights = (0.5 / PAIRS * (jnp.exp(scores - row_lse[:, None]) + jnp.exp(scores - col_lse[None, :])) - hit / PAIRS).astype(jnp.bfloat16)
    d_q = logit_scale * jnp.dot(weights, p_half, preferred_element_type=jnp.float32)
    d_p = logit_scale * jnp.dot(weights.T, q_half, preferred_element_type=jnp.float32)
    grad_queries = (d_q - q_unit * lax.optimization_barrier(jnp.sum(q_unit * d_q, axis=1))[:, None]) / q_norm[:, None]
    grad_paraphrases = (d_p - p_unit * lax.optimization_barrier(jnp.sum(p_unit * d_p, axis=1))[:, None]) / p_norm[:, None]
    return (loss, grad_queries.astype(jnp.bfloat16), grad_paraphrases.astype(jnp.bfloat16))
```

```python
import functools

import jax
import jax.numpy as jnp
from jax import lax
from jax.experimental import pallas as pl
from jax.experimental.pallas import tpu as pltpu
from jax.sharding import PartitionSpec as P

MESH = pl.DeviceIdType.MESH
F32 = jnp.float32
BF16 = jnp.bfloat16
GRID = (2, 8, 8)
NT = (((1,), (1,)), ((), ()))
NN = (((1,), (0,)), ((), ()))
OWN_Q, OWN_P, SWAP_Q, SWAP_P, FAR_Q, FAR_P, CORE, CHIP, ROWS, COLS, GRAD_Q, GRAD_P = range(12)


def dot(a, b, dims):
    return lax.dot_general(a, b, dims, preferred_element_type=F32)


def column(row):
    n = row.shape[1]
    return jnp.broadcast_to(row, (n, n)).T


def farthest_first(n):
    return sorted(range(1, n), key=lambda t: -min(t, n - t))


def kernel(grid, scale_ref, partner_any, q_any, p_any, loss_ref, gq_ref, gp_ref,
           partner_ref, q_in, p_in, qb, pb, qn, pn, part, part_core, half_sum, part_chip,
           row_stat, row_stats, col_stat, col_stats, gq, rq, gp, rp, load, send, recv):
    _, gy, gz = grid
    rows, feats = q_in.shape
    half = feats // 2
    nz, ny = gz * rows, gy * rows
    pairs = 2 * gy * nz
    b, m = lax.axis_index("batch"), lax.axis_index("mp")
    x, y, z = b // (gy * gz), b // gz % gy, b % gz

    z_peers = {t: (z + t) % gz for t in farthest_first(gz)}
    y_peers = {t: (y + t) % gy for t in farthest_first(gy)}
    z_peers = [(i, {"batch": (x * gy + y) * gz + i}) for i in z_peers.values()]
    y_peers = [(i, {"batch": (x * gy + i) * gz + z}) for i in y_peers.values()]
    x_peer = {"batch": ((1 - x) * gy + y) * gz + z}
    core_peer = {"mp": m // 2 * 2 + (m + 1) % 2}
    chip_peer = {"mp": (m + 2) % 4}

    barrier = pltpu.get_barrier_semaphore()
    everyone = [d for _, d in z_peers + y_peers] + [x_peer, chip_peer, core_peer]
    for d in everyone:
        pl.semaphore_signal(barrier, inc=1, device_id=d, device_id_type=MESH)
    loads = [
        pltpu.make_async_copy(source, target, load.at[i])
        for i, (source, target) in enumerate(
            ((q_any, q_in), (p_any, p_in), (partner_any, partner_ref))
        )
    ]
    for copy in loads:
        copy.start()

    def slot(ref, index, size=16):
        return ref.at[pl.ds(pl.multiple_of(index * size, size), size)]

    sent = []

    def push(src, dst, s, device):
        copy = pltpu.make_async_remote_copy(
            src_ref=src, dst_ref=dst, send_sem=send.at[s], recv_sem=recv.at[s],
            device_id=device, device_id_type=MESH,
        )
        copy.start()

    def arrived(ref, s, count, size):
        view = ref.at[pl.ds(0, count * size)]
        pltpu.make_async_copy(view, view, recv.at[s]).wait()
        sent.append((view, s))

    def halves(ref):
        whole = ref[...].astype(F32)
        return jnp.concatenate([whole[:, :half], whole[:, half:]], axis=0)

    for copy in loads:
        copy.wait()
    place = lax.broadcasted_iota(jnp.int32, (16, 128), 0)
    tag = jnp.zeros((16, 128), jnp.int32)
    for i in range(rows):
        tag = jnp.where(place == i, partner_ref[i] // 32, tag)
        tag = jnp.where(place == rows + i, partner_ref[i] % 32, tag)
    slot(qb, z)[...] = jnp.concatenate([halves(q_in), tag.astype(F32)], axis=1).astype(BF16)
    slot(pb, y)[...] = halves(p_in).astype(BF16)
    pl.semaphore_wait(barrier, len(everyone))

    push(slot(qb, z), slot(qb, gz + z), SWAP_Q, x_peer)
    push(slot(pb, y), slot(pb, gy + y), SWAP_P, x_peer)
    for t in range(max(gy, gz) - 1):
        if t < gz - 1:
            push(slot(qb, z), slot(qb, z), OWN_Q, z_peers[t][1])
        if t < gy - 1:
            push(slot(pb, y), slot(pb, y), OWN_P, y_peers[t][1])
    arrived(qb, SWAP_Q, 1, 16)
    arrived(pb, SWAP_P, 1, 16)
    for t in range(max(gy, gz) - 1):
        if t < gz - 1:
            push(slot(qb, gz + z), slot(qb, gz + z), FAR_Q, z_peers[t][1])
        if t < gy - 1:
            push(slot(pb, gy + y), slot(pb, gy + y), FAR_P, y_peers[t][1])

    def unpack(ref, out, r, n):
        whole = ref[r * n * 16:(r + 1) * n * 16, :half].astype(F32).reshape(n, 2, 8, half)
        whole = jnp.concatenate([whole[:, 0], whole[:, 1]], axis=2).reshape(n * 8, feats)
        out[r * n * 8:(r + 1) * n * 8, :] = whole.astype(BF16)
        square = whole * whole
        width = min(128, feats)
        return sum(square[:, c:c + width] for c in range(0, feats, width))

    arrived(qb, OWN_Q, gz - 1, 16)
    q_near = unpack(qb, qn, 0, gz)
    arrived(pb, OWN_P, gy - 1, 16)
    p_near = unpack(pb, pn, 0, gy)
    arrived(qb, FAR_Q, gz - 1, 16)
    q_far = unpack(qb, qn, 1, gz)
    arrived(pb, FAR_P, gy - 1, 16)
    p_far = unpack(pb, pn, 1, gy)

    q_sum = jnp.sum(jnp.concatenate([q_near, q_far], axis=0).T, axis=0, keepdims=True)
    p_sum = jnp.sum(jnp.concatenate([p_near, p_far], axis=0).T, axis=0, keepdims=True)
    part[0:2 * nz, :] = dot(qn[...], pn[...], NT)
    tile = lax.broadcasted_iota(jnp.int32, (8, 2 * ny), 0)
    part[2 * nz:2 * nz + 8, :] = jnp.where(tile == 0, q_sum, p_sum)
    size = 2 * nz + 8
    push(part, part_core, CORE, core_peer)
    arrived(part_core, CORE, 1, size)
    half_sum[...] = part[...] + part_core[...]
    push(half_sum, part_chip, CHIP, chip_peer)
    tags = qb[:, half:].astype(F32).reshape(2 * gz, 2, 8, 128)
    partner = (tags[:, 0] * 32.0 + tags[:, 1]).reshape(2 * nz, 128)[:, :2 * ny]
    lane = lax.broadcasted_iota(jnp.int32, (1, 2 * ny), 1)
    columns = (((x + lane // ny) % 2 * gy + lane // rows % gy) * gz + z) * rows + lane % rows
    hit = partner == columns.astype(F32)
    arrived(part_chip, CHIP, 1, size)
    total = half_sum[...] + part_chip[...]

    scale = scale_ref[0]
    q_inv = column(lax.rsqrt(total[2 * nz:2 * nz + 1] + 1e-6))
    p_inv = lax.rsqrt(total[2 * nz + 1:2 * nz + 2] + 1e-6)
    scores = (total[:2 * nz] * q_inv) * p_inv * scale
    across = scores.T

    def added(value, n):
        return jnp.sum(value[:n], axis=0, keepdims=True) + jnp.sum(value[n:], axis=0, keepdims=True)

    def both(row, n):
        return jnp.sum(row[:, :n]) + jnp.sum(row[:, n:])

    row_max = jnp.max(across, axis=0, keepdims=True)
    row_sum = added(jnp.exp(across - row_max), ny)
    col_max = jnp.max(scores, axis=0, keepdims=True)
    col_sum = added(jnp.exp(scores - col_max), nz)
    held = jnp.where(hit, scores, 0.0)
    near, far = (jnp.sum(held[r:r + nz], axis=0, keepdims=True) for r in (0, nz))
    hits = (jnp.sum(near[:, :ny]) + jnp.sum(far[:, ny:])) + (jnp.sum(near[:, ny:]) + jnp.sum(far[:, :ny]))
    stat = lax.broadcasted_iota(jnp.int32, (8, 2 * nz), 0)
    row_stat[...] = jnp.where(stat == 0, row_max, jnp.where(stat == 1, row_sum, hits))
    stat = lax.broadcasted_iota(jnp.int32, (8, 2 * ny), 0)
    col_stat[...] = jnp.where(stat == 0, col_max, col_sum)
    for t in range(max(gy, gz) - 1):
        if t < gz - 1:
            push(row_stat, slot(row_stats, z, 8), ROWS, z_peers[t][1])
        if t < gy - 1:
            push(col_stat, slot(col_stats, y, 8), COLS, y_peers[t][1])
    slot(row_stats, z, 8)[...] = row_stat[...]
    slot(col_stats, y, 8)[...] = col_stat[...]
    p_inv_col = column(p_inv)[:ny, :1]
    q_inv_col = q_inv[:nz, :1]

    def lse(ref, n):
        stats = ref[...].reshape(n, 8, ref.shape[1])
        most = jnp.max(stats[:, 0:1], axis=0)
        summed = jnp.sum(stats[:, 1:2] * jnp.exp(stats[:, 0:1] - most), axis=0)
        return most + jnp.log(summed), stats

    arrived(row_stats, ROWS, gz - 1, 8)
    row_lse, stats = lse(row_stats, gz)
    row_lse_col = column(row_lse)
    arrived(col_stats, COLS, gy - 1, 8)
    col_lse, _ = lse(col_stats, gy)

    weights = 0.5 / pairs * (jnp.exp(scores - row_lse_col) + jnp.exp(scores - col_lse))
    weights = weights - jnp.where(hit, 1.0 / pairs, 0.0)
    weights = weights.astype(BF16).astype(F32)
    turned = weights.T[:ny]
    weights = weights[:nz]

    def share(weight, score, other_inv, other, mine, mine_inv):
        n = weight.shape[0]
        scaled = weight * (scale * other_inv)
        high = scaled.astype(BF16).astype(F32)
        twice = jnp.concatenate([high, scaled - high], axis=0).astype(BF16)
        d = dot(twice, other, NN)
        along = jnp.sum(weight * score, axis=1, keepdims=True)
        d = (d[:n] + d[n:] - mine.astype(F32) * (along * mine_inv)) * mine_inv
        d = d.reshape(n // 8, 8, feats)
        return jnp.concatenate([d[:, :, :half], d[:, :, half:]], axis=1).reshape(n * 2, half)

    def extra(value, n):
        high = value.astype(BF16).astype(F32)
        middle = (value - high).astype(BF16).astype(F32)
        low = value - high - middle
        ext = jnp.where(place == 0, high, 0.0)
        ext = jnp.where(place == 1, middle, ext)
        ext = jnp.where(place == 2, low, ext).astype(BF16)
        return jnp.broadcast_to(ext[None], (n, 16, 128)).reshape(n * 16, 128)

    positives = jnp.sum(stats[:, 2:3, 0:1])
    gq[:, :half] = share(weights, scores[:nz], p_inv, pn[...], qn[0:nz, :], q_inv_col).astype(BF16)
    gq[:, half:] = extra(jnp.full((16, 128), 0.5 * both(col_lse, ny)), gz)
    for i, device in z_peers:
        push(slot(gq, i), slot(rq, z), GRAD_Q, device)
    slot(rq, z)[...] = slot(gq, z)[...]
    q_inv_row = lax.rsqrt(total[2 * nz:2 * nz + 1] + 1e-6)
    gp[:, :half] = share(turned, across[:ny], q_inv_row, qn[...], pn[0:ny, :], p_inv_col).astype(BF16)
    gp[:, half:] = extra(jnp.full((16, 128), 0.5 * both(row_lse, nz) - positives), gy)
    for i, device in y_peers:
        push(slot(gp, i), slot(rp, y), GRAD_P, device)
    slot(rp, y)[...] = slot(gp, y)[...]

    def gathered(ref, n, out_ref):
        whole = jnp.sum(ref[...].astype(F32).reshape(n, 16, half + 128), axis=0)
        out_ref[...] = jnp.concatenate([whole[:8, :half], whole[8:, :half]], axis=1).astype(BF16)
        return jnp.sum(whole[:, half:half + 1])

    arrived(rq, GRAD_Q, gz - 1, 16)
    loss = gathered(rq, gz, gq_ref)
    arrived(rp, GRAD_P, gy - 1, 16)
    loss_ref[0] = (loss + gathered(rp, gy, gp_ref)) / pairs
    for view, s in sent:
        pltpu.make_async_copy(view, view, send.at[s]).wait()


def build(mesh, grid):
    _, gy, gz = grid

    def shards(queries, paraphrases, partner, logit_scale):
        rows, feats = queries.shape
        half = feats // 2
        nz, ny = gz * rows, gy * rows
        vmem, smem = pl.BlockSpec(memory_space=pltpu.VMEM), pl.BlockSpec(memory_space=pltpu.SMEM)
        anywhere = pl.BlockSpec(memory_space=pl.ANY)
        block = pltpu.VMEM((2 * nz + 8, 2 * ny), F32)
        loss, grad_q, grad_p = pl.pallas_call(
            functools.partial(kernel, grid),
            out_shape=(
                jax.ShapeDtypeStruct((1,), F32),
                jax.ShapeDtypeStruct((rows, feats), BF16),
                jax.ShapeDtypeStruct((rows, feats), BF16),
            ),
            in_specs=[smem, anywhere, anywhere, anywhere],
            out_specs=(smem, vmem, vmem),
            scratch_shapes=[
                pltpu.SMEM((rows,), jnp.int32),
                pltpu.VMEM((rows, feats), BF16),
                pltpu.VMEM((rows, feats), BF16),
                pltpu.VMEM((gz * 32, half + 128), BF16),
                pltpu.VMEM((gy * 32, half), BF16),
                pltpu.VMEM((2 * nz, feats), BF16),
                pltpu.VMEM((2 * ny, feats), BF16),
                block,
                block,
                block,
                block,
                pltpu.VMEM((8, 2 * nz), F32),
                pltpu.VMEM((gz * 8, 2 * nz), F32),
                pltpu.VMEM((8, 2 * ny), F32),
                pltpu.VMEM((gy * 8, 2 * ny), F32),
                pltpu.VMEM((gz * 16, half + 128), BF16),
                pltpu.VMEM((gz * 16, half + 128), BF16),
                pltpu.VMEM((gy * 16, half + 128), BF16),
                pltpu.VMEM((gy * 16, half + 128), BF16),
                pltpu.SemaphoreType.DMA((3,)),
                pltpu.SemaphoreType.DMA((12,)),
                pltpu.SemaphoreType.DMA((12,)),
            ],
            compiler_params=pltpu.CompilerParams(
                collective_id=0, has_side_effects=True, vmem_limit_bytes=32 * 1024 * 1024
            ),
        )(logit_scale.reshape(1), partner, queries, paraphrases)
        return loss[0], grad_q, grad_p

    if mesh is None:
        return shards
    return jax.shard_map(
        shards,
        mesh=mesh,
        in_specs=(P("batch", "mp"), P("batch", "mp"), P("batch"), P()),
        out_specs=(P(), P("batch", "mp"), P("batch", "mp")),
        check_vma=False,
    )


def solution(mesh):
    return build(mesh, GRID)
```

```python
import functools

import jax
import jax.numpy as jnp
from jax import lax
from jax.experimental import pallas as pl
from jax.experimental.pallas import tpu as pltpu
from jax.sharding import PartitionSpec as P

MESH = pl.DeviceIdType.MESH
F32 = jnp.float32
BF16 = jnp.bfloat16
GRID = (2, 8, 8)
NT = (((1,), (1,)), ((), ()))
NN = (((1,), (0,)), ((), ()))
OWN_Q, OWN_P, SWAP_Q, SWAP_P, FAR_Q, FAR_P, CORE, LEFT, RIGHT, ROWS, COLS, GRAD_Q, GRAD_P = range(13)


def dot(a, b, dims):
    return lax.dot_general(a, b, dims, preferred_element_type=F32)


def column(row):
    n = row.shape[1]
    return jnp.broadcast_to(row, (n, n)).T


def farthest_first(n):
    return sorted(range(1, n), key=lambda t: -min(t, n - t))


def kernel(grid, scale_any, partner_any, q_any, p_any, rq, rp,
           scale_ref, partner_ref, q_in, p_in, qb, pb, qn, pn, part, part_core, part_left, part_right,
           row_stat, row_stats, col_stat, col_stats, gq, gp, load, send, recv):
    _, gy, gz = grid
    rows, feats = q_in.shape
    half = feats // 2
    nz, ny = gz * rows, gy * rows
    pairs = 2 * gy * nz
    b, m = lax.axis_index("batch"), lax.axis_index("mp")
    x, y, z = b // (gy * gz), b // gz % gy, b % gz

    z_peers = {t: (z + t) % gz for t in farthest_first(gz)}
    y_peers = {t: (y + t) % gy for t in farthest_first(gy)}
    z_peers = [(i, {"batch": (x * gy + y) * gz + i}) for i in z_peers.values()]
    y_peers = [(i, {"batch": (x * gy + i) * gz + z}) for i in y_peers.values()]
    x_peer = {"batch": ((1 - x) * gy + y) * gz + z}
    core, other = m % 2, (m + 2) % 4 // 2 * 2
    core_peer = {"mp": m // 2 * 2 + (m + 1) % 2}
    left_peers = [{"mp": other + c} for c in range(2)]
    right_peers = [{"batch": x_peer["batch"], "mp": other + c} for c in range(2)]

    barrier = pltpu.get_barrier_semaphore()
    everyone = [d for _, d in z_peers + y_peers] + [x_peer, *left_peers, *right_peers, core_peer]
    for d in everyone:
        pl.semaphore_signal(barrier, inc=1, device_id=d, device_id_type=MESH)
    loads = [
        pltpu.make_async_copy(source, target, load.at[i])
        for i, (source, target) in enumerate(
            ((q_any, q_in), (p_any, p_in), (partner_any, partner_ref), (scale_any, scale_ref))
        )
    ]
    for copy in loads:
        copy.start()

    def slot(ref, index, size=16):
        return ref.at[pl.ds(pl.multiple_of(index * size, size), size)]

    sent = []

    def push(src, dst, s, device):
        copy = pltpu.make_async_remote_copy(
            src_ref=src, dst_ref=dst, send_sem=send.at[s], recv_sem=recv.at[s],
            device_id=device, device_id_type=MESH,
        )
        copy.start()

    def arrived(ref, s, count, size):
        view = ref.at[pl.ds(0, count * size)]
        pltpu.make_async_copy(view, view, recv.at[s]).wait()
        sent.append((view, s))

    def halves(ref):
        whole = ref[...].astype(F32)
        return jnp.concatenate([whole[:, :half], whole[:, half:]], axis=0)

    for copy in loads:
        copy.wait()
    place = lax.broadcasted_iota(jnp.int32, (16, 128), 0)
    tag = jnp.zeros((16, 128), jnp.int32)
    for i in range(rows):
        tag = jnp.where(place == i, partner_ref[i] // 32, tag)
        tag = jnp.where(place == rows + i, partner_ref[i] % 32, tag)
    slot(qb, z)[...] = jnp.concatenate([halves(q_in), tag.astype(F32)], axis=1).astype(BF16)
    slot(pb, y)[...] = halves(p_in).astype(BF16)
    pl.semaphore_wait(barrier, len(everyone))

    push(slot(qb, z), slot(qb, gz + z), SWAP_Q, x_peer)
    push(slot(pb, y), slot(pb, gy + y), SWAP_P, x_peer)
    for t in range(max(gy, gz) - 1):
        if t < gz - 1:
            push(slot(qb, z), slot(qb, z), OWN_Q, z_peers[t][1])
        if t < gy - 1:
            push(slot(pb, y), slot(pb, y), OWN_P, y_peers[t][1])
    arrived(qb, SWAP_Q, 1, 16)
    arrived(pb, SWAP_P, 1, 16)
    for t in range(max(gy, gz) - 1):
        if t < gz - 1:
            push(slot(qb, gz + z), slot(qb, gz + z), FAR_Q, z_peers[t][1])
        if t < gy - 1:
            push(slot(pb, gy + y), slot(pb, gy + y), FAR_P, y_peers[t][1])

    def unpack(ref, out, r, n):
        whole = ref[r * n * 16:(r + 1) * n * 16, :half].astype(F32).reshape(n, 2, 8, half)
        whole = jnp.concatenate([whole[:, 0], whole[:, 1]], axis=2).reshape(n * 8, feats)
        out[r * n * 8:(r + 1) * n * 8, :] = whole.astype(BF16)
        square = whole * whole
        width = min(128, feats)
        return sum(square[:, c:c + width] for c in range(0, feats, width))

    arrived(qb, OWN_Q, gz - 1, 16)
    q_near = unpack(qb, qn, 0, gz)
    arrived(pb, OWN_P, gy - 1, 16)
    p_near = unpack(pb, pn, 0, gy)
    arrived(qb, FAR_Q, gz - 1, 16)
    q_far = unpack(qb, qn, 1, gz)
    arrived(pb, FAR_P, gy - 1, 16)
    p_far = unpack(pb, pn, 1, gy)

    q_sum = jnp.sum(jnp.concatenate([q_near, q_far], axis=0).T, axis=0, keepdims=True)
    p_sum = jnp.sum(jnp.concatenate([p_near, p_far], axis=0).T, axis=0, keepdims=True)
    part[0:nz, :] = dot(qn[nz:, :], pn[...], NT)
    part[nz:2 * nz, :] = dot(qn[0:nz, :], pn[...], NT)
    tile = lax.broadcasted_iota(jnp.int32, (8, 2 * ny), 0)
    part[2 * nz:2 * nz + 8, :] = jnp.where(tile == 0, q_sum, p_sum)
    size = 2 * nz + 8
    for device in left_peers:
        push(part.at[pl.ds(nz, nz + 8)], slot(part_left, core, nz + 8), LEFT, device)
    for device in right_peers:
        push(part.at[pl.ds(nz, nz)], slot(part_right, core, nz), RIGHT, device)
    push(part, part_core, CORE, core_peer)
    tags = qb[:, half:].astype(F32).reshape(2 * gz, 2, 8, 128)
    partner = (tags[:, 0] * 32.0 + tags[:, 1]).reshape(2 * nz, 128)[:, :2 * ny]
    lane = lax.broadcasted_iota(jnp.int32, (1, 2 * ny), 1)
    columns = (((x + lane // ny) % 2 * gy + lane // rows % gy) * gz + z) * rows + lane % rows
    hit = partner == columns.astype(F32)
    arrived(part_core, CORE, 1, size)
    total = part[...] + part_core[...]
    arrived(part_left, LEFT, 2, nz + 8)
    left = part_left[0:nz + 8, :] + part_left[nz + 8:, :]
    arrived(part_right, RIGHT, 2, nz)
    right = pltpu.roll(part_right[0:nz, :] + part_right[nz:, :], ny, 1)
    total = total + jnp.concatenate([right, left], axis=0)

    scale = scale_ref[0]
    q_inv = column(lax.rsqrt(total[2 * nz:2 * nz + 1] + 1e-6))
    p_inv = lax.rsqrt(total[2 * nz + 1:2 * nz + 2] + 1e-6)
    product = jnp.concatenate([total[nz:2 * nz], total[:nz]], axis=0)
    scores = (product * q_inv) * p_inv * scale
    across = scores.T

    def added(value, n):
        return jnp.sum(value[:n], axis=0, keepdims=True) + jnp.sum(value[n:], axis=0, keepdims=True)

    def both(row, n):
        return jnp.sum(row[:, :n]) + jnp.sum(row[:, n:])

    row_max = jnp.max(across, axis=0, keepdims=True)
    row_sum = added(jnp.exp(across - row_max), ny)
    col_max = jnp.max(scores, axis=0, keepdims=True)
    col_sum = added(jnp.exp(scores - col_max), nz)
    held = jnp.where(hit, scores, 0.0)
    near, far = (jnp.sum(held[r:r + nz], axis=0, keepdims=True) for r in (0, nz))
    hits = (jnp.sum(near[:, :ny]) + jnp.sum(far[:, ny:])) + (jnp.sum(near[:, ny:]) + jnp.sum(far[:, :ny]))
    stat = lax.broadcasted_iota(jnp.int32, (8, 2 * nz), 0)
    row_stat[...] = jnp.where(stat == 0, row_max, jnp.where(stat == 1, row_sum, hits))
    stat = lax.broadcasted_iota(jnp.int32, (8, 2 * ny), 0)
    col_stat[...] = jnp.where(stat == 0, col_max, col_sum)
    for t in range(max(gy, gz) - 1):
        if t < gz - 1:
            push(row_stat, slot(row_stats, z, 8), ROWS, z_peers[t][1])
        if t < gy - 1:
            push(col_stat, slot(col_stats, y, 8), COLS, y_peers[t][1])
    slot(row_stats, z, 8)[...] = row_stat[...]
    slot(col_stats, y, 8)[...] = col_stat[...]
    p_inv_col = column(p_inv)[:ny, :1]
    q_inv_col = q_inv[:nz, :1]

    def lse(ref, n):
        stats = ref[...].reshape(n, 8, ref.shape[1])
        most = jnp.max(stats[:, 0:1], axis=0)
        summed = jnp.sum(stats[:, 1:2] * jnp.exp(stats[:, 0:1] - most), axis=0)
        return most + jnp.log(summed), stats

    arrived(row_stats, ROWS, gz - 1, 8)
    row_lse, stats = lse(row_stats, gz)
    row_lse_col = column(row_lse)
    arrived(col_stats, COLS, gy - 1, 8)
    col_lse, _ = lse(col_stats, gy)

    weights = 0.5 / pairs * (jnp.exp(scores - row_lse_col) + jnp.exp(scores - col_lse))
    weights = weights - jnp.where(hit, 1.0 / pairs, 0.0)
    weights = weights.astype(BF16).astype(F32)
    turned = weights.T[:ny]
    weights = weights[:nz]

    def share(weight, score, other_inv, other, mine, mine_inv):
        n = weight.shape[0]
        scaled = weight * (scale * other_inv)
        high = scaled.astype(BF16).astype(F32)
        twice = jnp.concatenate([high, scaled - high], axis=0).astype(BF16)
        d = dot(twice, other, NN)
        along = jnp.sum(weight * score, axis=1, keepdims=True)
        d = (d[:n] + d[n:] - mine.astype(F32) * (along * mine_inv)) * mine_inv
        d = d.reshape(n // 8, 8, feats)
        return jnp.concatenate([d[:, :, :half], d[:, :, half:]], axis=1).reshape(n * 2, half)

    def extra(value, n):
        high = value.astype(BF16).astype(F32)
        middle = (value - high).astype(BF16).astype(F32)
        low = value - high - middle
        ext = jnp.where(place == 0, high, 0.0)
        ext = jnp.where(place == 1, middle, ext)
        ext = jnp.where(place == 2, low, ext).astype(BF16)
        return jnp.broadcast_to(ext[None], (n, 16, 128)).reshape(n * 16, 128)

    positives = jnp.sum(stats[:, 2:3, 0:1])
    gq[:, :half] = share(weights, scores[:nz], p_inv, pn[...], qn[0:nz, :], q_inv_col).astype(BF16)
    gq[:, half:] = extra(jnp.full((16, 128), 0.5 * both(col_lse, ny)), gz)
    for i, device in z_peers:
        push(slot(gq, i), slot(rq, z), GRAD_Q, device)
    keep_q = pltpu.make_async_copy(slot(gq, z), slot(rq, z), load.at[0])
    keep_q.start()
    q_inv_row = lax.rsqrt(total[2 * nz:2 * nz + 1] + 1e-6)
    gp[:, :half] = share(turned, across[:ny], q_inv_row, qn[...], pn[0:ny, :], p_inv_col).astype(BF16)
    gp[:, half:] = extra(jnp.full((16, 128), 0.5 * both(row_lse, nz) - positives), gy)
    for i, device in y_peers:
        push(slot(gp, i), slot(rp, y), GRAD_P, device)
    keep_p = pltpu.make_async_copy(slot(gp, y), slot(rp, y), load.at[1])
    keep_p.start()

    keep_q.wait()
    keep_p.wait()
    arrived(rq, GRAD_Q, gz - 1, 16)
    arrived(rp, GRAD_P, gy - 1, 16)
    for view, s in sent:
        pltpu.make_async_copy(view, view, send.at[s]).wait()


def finish(pairs, rq, rp, loss_ref, gq_ref, gp_ref):
    half = gq_ref.shape[1] // 2

    def gathered(ref, out_ref):
        whole = jnp.sum(ref[...].astype(F32).reshape(-1, 16, half + 128), axis=0)
        out_ref[...] = jnp.concatenate([whole[:8, :half], whole[8:, :half]], axis=1).astype(BF16)
        return jnp.sum(whole[:, half:half + 1])

    loss_ref[0] = (gathered(rq, gq_ref) + gathered(rp, gp_ref)) / pairs


def build(mesh, grid):
    _, gy, gz = grid

    def shards(queries, paraphrases, partner, logit_scale):
        rows, feats = queries.shape
        half = feats // 2
        nz, ny = gz * rows, gy * rows
        vmem, smem = pl.BlockSpec(memory_space=pltpu.VMEM), pl.BlockSpec(memory_space=pltpu.SMEM)
        anywhere = pl.BlockSpec(memory_space=pl.ANY)
        block = pltpu.VMEM((2 * nz + 8, 2 * ny), F32)
        shares_q, shares_p = pl.pallas_call(
            functools.partial(kernel, grid),
            out_shape=(
                jax.ShapeDtypeStruct((gz * 16, half + 128), BF16),
                jax.ShapeDtypeStruct((gy * 16, half + 128), BF16),
            ),
            in_specs=[anywhere] * 4,
            out_specs=(anywhere, anywhere),
            scratch_shapes=[
                pltpu.SMEM((1,), F32),
                pltpu.SMEM((rows,), jnp.int32),
                pltpu.VMEM((rows, feats), BF16),
                pltpu.VMEM((rows, feats), BF16),
                pltpu.VMEM((gz * 32, half + 128), BF16),
                pltpu.VMEM((gy * 32, half), BF16),
                pltpu.VMEM((2 * nz, feats), BF16),
                pltpu.VMEM((2 * ny, feats), BF16),
                block,
                block,
                pltpu.VMEM((2 * (nz + 8), 2 * ny), F32),
                pltpu.VMEM((2 * nz, 2 * ny), F32),
                pltpu.VMEM((8, 2 * nz), F32),
                pltpu.VMEM((gz * 8, 2 * nz), F32),
                pltpu.VMEM((8, 2 * ny), F32),
                pltpu.VMEM((gy * 8, 2 * ny), F32),
                pltpu.VMEM((gz * 16, half + 128), BF16),
                pltpu.VMEM((gy * 16, half + 128), BF16),
                pltpu.SemaphoreType.DMA((4,)),
                pltpu.SemaphoreType.DMA((13,)),
                pltpu.SemaphoreType.DMA((13,)),
            ],
            compiler_params=pltpu.CompilerParams(
                collective_id=0, has_side_effects=True, vmem_limit_bytes=60 * 1024 * 1024
            ),
        )(logit_scale.reshape(1), partner, queries, paraphrases)
        loss, grad_q, grad_p = pl.pallas_call(
            functools.partial(finish, 2 * gy * nz),
            out_shape=(
                jax.ShapeDtypeStruct((1,), F32),
                jax.ShapeDtypeStruct((rows, feats), BF16),
                jax.ShapeDtypeStruct((rows, feats), BF16),
            ),
            in_specs=[vmem, vmem],
            out_specs=(smem, vmem, vmem),
            compiler_params=pltpu.CompilerParams(vmem_limit_bytes=60 * 1024 * 1024),
        )(shares_q, shares_p)
        return loss[0], grad_q, grad_p

    if mesh is None:
        return shards
    return jax.shard_map(
        shards,
        mesh=mesh,
        in_specs=(P("batch", "mp"), P("batch", "mp"), P("batch"), P()),
        out_specs=(P(), P("batch", "mp"), P("batch", "mp")),
        check_vma=False,
    )


def solution(mesh):
    return build(mesh, GRID)
```

```python
import functools

import jax
import jax.numpy as jnp
from jax import lax
from jax.experimental import pallas as pl
from jax.experimental.pallas import tpu as pltpu
from jax.sharding import PartitionSpec as P

MESH = pl.DeviceIdType.MESH
F32 = jnp.float32
BF16 = jnp.bfloat16
GRID = (2, 8, 8)
NT = (((1,), (1,)), ((), ()))
NN = (((1,), (0,)), ((), ()))
OWN_Q, OWN_P, SWAP_Q, SWAP_P, FAR_Q, FAR_P, CORE, LEFT, RIGHT, ROWS, COLS, GRAD_Q, GRAD_P, OWN_T, SWAP_T, FAR_T,\
    CORE_E, LEFT_E, RIGHT_E, LOSS_Z, LOSS_Y = range(21)


def dot(a, b, dims):
    return lax.dot_general(a, b, dims, preferred_element_type=F32)


def column(row):
    n = row.shape[1]
    return jnp.broadcast_to(row, (n, n)).T


def farthest_first(n):
    return sorted(range(1, n), key=lambda t: -min(t, n - t))


def kernel(grid, scale_any, partner_any, q_any, p_any, rq, rp, loss_z, loss_y,
           scale_ref, partner_ref, q_in, p_in, qb, pb, qn, pn, part, part_core, part_left, part_right,
           first, first_core, first_left, first_right,
           row_stat, row_stats, col_stat, col_stats, gq, gp, tags, q_less, p_less, loss_part, load, send, recv):
    _, gy, gz = grid
    rows, feats = q_in.shape
    half = feats // 2
    nz, ny = gz * rows, gy * rows
    pairs = 2 * gy * nz
    b, m = lax.axis_index("batch"), lax.axis_index("mp")
    x, y, z = b // (gy * gz), b // gz % gy, b % gz

    z_peers = {t: (z + t) % gz for t in farthest_first(gz)}
    y_peers = {t: (y + t) % gy for t in farthest_first(gy)}
    z_peers = [(i, {"batch": (x * gy + y) * gz + i}) for i in z_peers.values()]
    y_peers = [(i, {"batch": (x * gy + i) * gz + z}) for i in y_peers.values()]
    x_peer = {"batch": ((1 - x) * gy + y) * gz + z}
    core, other = m % 2, (m + 2) % 4 // 2 * 2
    core_peer = {"mp": m // 2 * 2 + (m + 1) % 2}
    left_peers = [{"mp": other + c} for c in range(2)]
    right_peers = [{"batch": x_peer["batch"], "mp": other + c} for c in range(2)]

    loads = [
        pltpu.make_async_copy(source, target, load.at[i])
        for i, (source, target) in enumerate(
            ((q_any, q_in), (p_any, p_in), (partner_any, partner_ref), (scale_any, scale_ref))
        )
    ]
    for copy in loads:
        copy.start()
    barrier = pltpu.get_barrier_semaphore()
    everyone = [x_peer] + [d for pair in zip(z_peers, y_peers) for _, d in pair] + [*left_peers, *right_peers, core_peer]
    for d in everyone:
        pl.semaphore_signal(barrier, inc=1, device_id=d, device_id_type=MESH)

    def slot(ref, index, size=16):
        return ref.at[pl.ds(pl.multiple_of(index * size, size), size)]

    sent = []

    def push(src, dst, s, device):
        copy = pltpu.make_async_remote_copy(
            src_ref=src, dst_ref=dst, send_sem=send.at[s], recv_sem=recv.at[s],
            device_id=device, device_id_type=MESH,
        )
        copy.start()

    def arrived(ref, s, count, size):
        view = ref.at[pl.ds(0, count * size)]
        pltpu.make_async_copy(view, view, recv.at[s]).wait()
        sent.append((view, s))

    def halves(ref):
        whole = ref[...].astype(F32)
        return jnp.concatenate([whole[:, :half], whole[:, half:]], axis=0)

    loads[0].wait()
    slot(qb, z)[...] = halves(q_in).astype(BF16)
    loads[1].wait()
    slot(pb, y)[...] = halves(p_in).astype(BF16)
    pl.semaphore_wait(barrier, len(everyone))

    push(slot(qb, z), slot(qb, gz + z), SWAP_Q, x_peer)
    push(slot(pb, y), slot(pb, gy + y), SWAP_P, x_peer)
    for t in range(max(gy, gz) - 1):
        if t < gz - 1:
            push(slot(qb, z), slot(qb, z), OWN_Q, z_peers[t][1])
        if t < gy - 1:
            push(slot(pb, y), slot(pb, y), OWN_P, y_peers[t][1])

    loads[2].wait()
    loads[3].wait()
    spot = lax.broadcasted_iota(jnp.int32, (1, 1, 2 * nz), 2) % rows
    tag = jnp.zeros((1, 1, 2 * nz), jnp.int32)
    for i in range(rows):
        tag = jnp.where(spot == i, partner_ref[i], tag)
    tags[pl.ds(z, 1)] = tag.astype(F32)
    push(tags.at[pl.ds(z, 1)], tags.at[pl.ds(gz + z, 1)], SWAP_T, x_peer)

    arrived(qb, SWAP_Q, 1, 16)
    for _, device in z_peers[:3]:
        push(slot(qb, gz + z), slot(qb, gz + z), FAR_Q, device)
    arrived(pb, SWAP_P, 1, 16)
    for _, device in y_peers[:3]:
        push(slot(pb, gy + y), slot(pb, gy + y), FAR_P, device)
    for t in range(3, max(gy, gz) - 1):
        if t < gz - 1:
            push(slot(qb, gz + z), slot(qb, gz + z), FAR_Q, z_peers[t][1])
        if t < gy - 1:
            push(slot(pb, gy + y), slot(pb, gy + y), FAR_P, y_peers[t][1])
    arrived(tags, SWAP_T, 1, 1)
    for _, device in z_peers:
        push(tags.at[pl.ds(z, 1)], tags.at[pl.ds(z, 1)], OWN_T, device)
        push(tags.at[pl.ds(gz + z, 1)], tags.at[pl.ds(gz + z, 1)], FAR_T, device)

    def unpack(ref, out, r, n):
        whole = ref[r * n * 16:(r + 1) * n * 16, :half].astype(F32).reshape(n, 2, 8, half)
        whole = jnp.concatenate([whole[:, 0], whole[:, 1]], axis=2).reshape(n * 8, feats)
        out[r * n * 8:(r + 1) * n * 8, :] = whole.astype(BF16)
        square = whole * whole
        width = min(128, feats)
        return sum(square[:, c:c + width] for c in range(0, feats, width))

    arrived(qb, OWN_Q, gz - 1, 16)
    q_near = unpack(qb, qn, 0, gz)
    arrived(pb, OWN_P, gy - 1, 16)
    p_near = unpack(pb, pn, 0, gy)
    nh = nz // 2

    def fold(value):
        return jnp.concatenate([value[:nh], value[nh:]], axis=1)

    first[...] = fold(dot(qn[0:nz, :], pn[0:ny, :], NT))
    for device in left_peers:
        push(first, slot(first_left, core, nh), LEFT_E, device)
    for device in right_peers:
        push(first, slot(first_right, core, nh), RIGHT_E, device)
    push(first, first_core, CORE_E, core_peer)
    arrived(qb, FAR_Q, gz - 1, 16)
    q_far = unpack(qb, qn, 1, gz)
    part[0:nh, :] = fold(dot(qn[nz:, :], pn[0:ny, :], NT))
    tile = lax.broadcasted_iota(jnp.int32, (8, 2 * ny), 0)
    q_sum = jnp.sum(jnp.concatenate([q_near, q_far], axis=0).T, axis=0, keepdims=True)
    arrived(pb, FAR_P, gy - 1, 16)
    p_far = unpack(pb, pn, 1, gy)

    beyond = dot(qn[...], pn[ny:, :], NT)
    part[2 * nh:3 * nh, :] = fold(beyond[:nz])
    p_sum = jnp.sum(jnp.concatenate([p_near, p_far], axis=0).T, axis=0, keepdims=True)
    part[3 * nh:3 * nh + 8, :] = jnp.where(tile == 0, q_sum, p_sum)
    for device in left_peers:
        push(part.at[pl.ds(2 * nh, nh + 8)], slot(part_left, core, nh + 8), LEFT, device)
    for device in right_peers:
        push(part.at[pl.ds(2 * nh, nh)], slot(part_right, core, nh), RIGHT, device)
    part[nh:2 * nh, :] = fold(beyond[nz:])
    push(part, part_core, CORE, core_peer)
    arrived(tags, OWN_T, gz - 1, 1)
    arrived(tags, FAR_T, gz - 1, 1)
    seat = lax.broadcasted_iota(jnp.int32, (2 * gz, 1, 2 * nz), 2) // rows
    taken = seat == lax.broadcasted_iota(jnp.int32, (2 * gz, 1, 2 * nz), 0)
    partner = column(jnp.sum(jnp.where(taken, tags[...], 0.0), axis=0))
    lane = lax.broadcasted_iota(jnp.int32, (1, 2 * ny), 1)
    columns = (((x + lane // ny) % 2 * gy + lane // rows % gy) * gz + z) * rows + lane % rows
    hit = partner == columns.astype(F32)
    arrived(first_core, CORE_E, 1, nh)
    arrived(first_left, LEFT_E, 2, nh)
    arrived(first_right, RIGHT_E, 2, nh)
    arrived(part_core, CORE, 1, 3 * nh + 8)
    near = (first[...] + first_core[...]) + (first_left[0:nh, :] + first_left[nh:, :])
    right_near = first_right[0:nh, :] + first_right[nh:, :]
    total = part[...] + part_core[...]
    arrived(part_left, LEFT, 2, nh + 8)
    left = total[2 * nh:] + (part_left[0:nh + 8, :] + part_left[nh + 8:, :])
    arrived(part_right, RIGHT, 2, nh)
    right = part_right[0:nh, :] + part_right[nh:, :]
    lower = lane < ny

    def beside(a, b):
        return jnp.concatenate(
            [jnp.where(lower, a, pltpu.roll(b, ny, 1)), jnp.where(lower, pltpu.roll(a, ny, 1), b)], axis=0
        )

    product = jnp.concatenate(
        [beside(near, left[:nh]), beside(total[:nh] + right, total[nh:2 * nh] + right_near)], axis=0
    )
    sums = left[nh:]

    scale = scale_ref[0]
    q_inv = column(lax.rsqrt(sums[0:1] + 1e-6))
    p_inv = lax.rsqrt(sums[1:2] + 1e-6)
    scores = (product * q_inv) * p_inv * scale
    across = scores.T

    def added(value, n):
        return jnp.sum(value[:n], axis=0, keepdims=True) + jnp.sum(value[n:], axis=0, keepdims=True)

    def both(row, n):
        return jnp.sum(row[:, :n]) + jnp.sum(row[:, n:])

    row_max = jnp.max(across, axis=0, keepdims=True)
    row_exp = jnp.exp(across - row_max)
    row_sum = added(row_exp, ny)
    col_max = jnp.max(scores, axis=0, keepdims=True)
    col_exp = jnp.exp(scores - col_max)
    col_sum = added(col_exp, nz)
    held = jnp.where(hit, scores, 0.0)
    near, far = (jnp.sum(held[r:r + nz], axis=0, keepdims=True) for r in (0, nz))
    hits = (jnp.sum(near[:, :ny]) + jnp.sum(far[:, ny:])) + (jnp.sum(near[:, ny:]) + jnp.sum(far[:, :ny]))
    for i, value in enumerate((row_max, row_sum, jnp.full((1, 2 * nz), hits))):
        row_stat[i] = value
    for i, value in enumerate((col_max, col_sum)):
        col_stat[i] = value
    for t in range(max(gy, gz) - 1):
        if t < gz - 1:
            push(row_stat, slot(row_stats, z, 3), ROWS, z_peers[t][1])
        if t < gy - 1:
            push(col_stat, slot(col_stats, y, 2), COLS, y_peers[t][1])
    slot(row_stats, z, 3)[...] = row_stat[...]
    slot(col_stats, y, 2)[...] = col_stat[...]

    def units(raw, inv, less, n):
        inv = inv[:, :1]
        unit = raw[...].astype(F32) * inv
        raw[...] = unit.astype(BF16)
        less[...] = unit[:n] * inv[:n]
        return scale * inv[:n]

    q_scale = units(qn, q_inv, q_less, nz)
    p_scale = units(pn, column(p_inv), p_less, ny)
    row_exp = row_exp.T * (0.5 / pairs)
    col_exp = col_exp * (0.5 / pairs)
    hit = jnp.where(hit, 1.0 / pairs, 0.0)

    def lse(ref, n):
        stats = ref[...].reshape(n, -1, 1, ref.shape[2])
        most = jnp.max(stats[:, 0], axis=0)
        summed = jnp.sum(stats[:, 1] * jnp.exp(stats[:, 0] - most), axis=0)
        return most + jnp.log(summed), stats

    arrived(row_stats, ROWS, gz - 1, 3)
    row_lse, stats = lse(row_stats, gz)
    row_part = column(jnp.exp(row_max - row_lse))
    arrived(col_stats, COLS, gy - 1, 2)
    col_lse, _ = lse(col_stats, gy)

    weights = row_exp * row_part + col_exp * jnp.exp(col_max - col_lse) - hit
    weights = weights.astype(BF16).astype(F32)
    turned = weights.T[:ny]
    weights = weights[:nz]

    def share(weight, score, other, scaled, less):
        n = weight.shape[0]
        d = dot(weight.astype(BF16), other, NN)
        along = jnp.sum(weight * score, axis=1, keepdims=True)
        d = (d * scaled - less * along).reshape(n // 8, 8, feats)
        return jnp.concatenate([d[:, :, :half], d[:, :, half:]], axis=1).reshape(n * 2, half)

    positives = jnp.sum(stats[:, 2, 0, 0:1])
    loss_part[0] = jnp.full((1, 128), 0.5 * both(col_lse, ny))
    loss_part[1] = jnp.full((1, 128), 0.5 * both(row_lse, nz) - positives)
    for _, device in z_peers:
        push(loss_part.at[pl.ds(0, 1)], loss_z.at[pl.ds(z, 1)], LOSS_Z, device)
    for _, device in y_peers:
        push(loss_part.at[pl.ds(1, 1)], loss_y.at[pl.ds(y, 1)], LOSS_Y, device)

    gq[...] = share(weights, scores[:nz], pn[...], q_scale, q_less[...]).astype(BF16)
    for i, device in z_peers[:3]:
        push(slot(gq, i), slot(rq, z), GRAD_Q, device)
    gp[...] = share(turned, across[:ny], qn[...], p_scale, p_less[...]).astype(BF16)
    for i, device in y_peers[:3]:
        push(slot(gp, i), slot(rp, y), GRAD_P, device)
    for t in range(3, max(gy, gz) - 1):
        if t < gz - 1:
            push(slot(gq, z_peers[t][0]), slot(rq, z), GRAD_Q, z_peers[t][1])
        if t < gy - 1:
            push(slot(gp, y_peers[t][0]), slot(rp, y), GRAD_P, y_peers[t][1])
    keeps = [
        pltpu.make_async_copy(source, target, load.at[i])
        for i, (source, target) in enumerate((
            (slot(gq, z), slot(rq, z)),
            (slot(gp, y), slot(rp, y)),
            (loss_part.at[pl.ds(0, 1)], loss_z.at[pl.ds(z, 1)]),
            (loss_part.at[pl.ds(1, 1)], loss_y.at[pl.ds(y, 1)]),
        ))
    ]
    for copy in keeps:
        copy.start()
    for copy in keeps:
        copy.wait()
    arrived(rq, GRAD_Q, gz - 1, 16)
    arrived(rp, GRAD_P, gy - 1, 16)
    arrived(loss_z, LOSS_Z, gz - 1, 1)
    arrived(loss_y, LOSS_Y, gy - 1, 1)
    for view, s in sent:
        pltpu.make_async_copy(view, view, send.at[s]).wait()


def finish(pairs, rq, rp, loss_z, loss_y, loss_ref, gq_ref, gp_ref):
    half = gq_ref.shape[1] // 2

    for ref, out_ref in ((rq, gq_ref), (rp, gp_ref)):
        whole = jnp.sum(ref[...].astype(F32).reshape(-1, 16, half), axis=0)
        out_ref[...] = jnp.concatenate([whole[:8], whole[8:]], axis=1).astype(BF16)
    parts = jnp.sum(loss_z[...], axis=0) + jnp.sum(loss_y[...], axis=0)
    loss_ref[0] = jnp.sum(parts[:, 0:1]) / pairs


def build(mesh, grid):
    _, gy, gz = grid

    def shards(queries, paraphrases, partner, logit_scale):
        rows, feats = queries.shape
        half = feats // 2
        nz, ny = gz * rows, gy * rows
        vmem, smem = pl.BlockSpec(memory_space=pltpu.VMEM), pl.BlockSpec(memory_space=pltpu.SMEM)
        anywhere = pl.BlockSpec(memory_space=pl.ANY)
        block = pltpu.VMEM((nz + nz // 2 + 8, 2 * ny), F32)
        shares = pl.pallas_call(
            functools.partial(kernel, grid),
            out_shape=(
                jax.ShapeDtypeStruct((gz * 16, half), BF16),
                jax.ShapeDtypeStruct((gy * 16, half), BF16),
                jax.ShapeDtypeStruct((gz, 1, 128), F32),
                jax.ShapeDtypeStruct((gy, 1, 128), F32),
            ),
            in_specs=[anywhere] * 4,
            out_specs=(anywhere,) * 4,
            scratch_shapes=[
                pltpu.SMEM((1,), F32),
                pltpu.SMEM((rows,), jnp.int32),
                pltpu.VMEM((rows, feats), BF16),
                pltpu.VMEM((rows, feats), BF16),
                pltpu.VMEM((gz * 32, half), BF16),
                pltpu.VMEM((gy * 32, half), BF16),
                pltpu.VMEM((2 * nz, feats), BF16),
                pltpu.VMEM((2 * ny, feats), BF16),
                block,
                block,
                pltpu.VMEM((nz + 16, 2 * ny), F32),
                pltpu.VMEM((nz, 2 * ny), F32),
                pltpu.VMEM((nz // 2, 2 * ny), F32),
                pltpu.VMEM((nz // 2, 2 * ny), F32),
                pltpu.VMEM((nz, 2 * ny), F32),
                pltpu.VMEM((nz, 2 * ny), F32),
                pltpu.VMEM((3, 1, 2 * nz), F32),
                pltpu.VMEM((gz * 3, 1, 2 * nz), F32),
                pltpu.VMEM((2, 1, 2 * ny), F32),
                pltpu.VMEM((gy * 2, 1, 2 * ny), F32),
                pltpu.VMEM((gz * 16, half), BF16),
                pltpu.VMEM((gy * 16, half), BF16),
                pltpu.VMEM((2 * gz, 1, 2 * nz), F32),
                pltpu.VMEM((nz, feats), F32),
                pltpu.VMEM((ny, feats), F32),
                pltpu.VMEM((2, 1, 128), F32),
                pltpu.SemaphoreType.DMA((4,)),
                pltpu.SemaphoreType.DMA((21,)),
                pltpu.SemaphoreType.DMA((21,)),
            ],
            compiler_params=pltpu.CompilerParams(
                collective_id=0, has_side_effects=True, vmem_limit_bytes=32 * 1024 * 1024
            ),
        )(logit_scale.reshape(1), pltpu.with_memory_space_constraint(partner, pltpu.HBM), pltpu.with_memory_space_constraint(queries, pltpu.HBM), pltpu.with_memory_space_constraint(paraphrases, pltpu.HBM))
        loss, grad_q, grad_p = pl.pallas_call(
            functools.partial(finish, 2 * gy * nz),
            out_shape=(
                jax.ShapeDtypeStruct((1,), F32),
                jax.ShapeDtypeStruct((rows, feats), BF16),
                jax.ShapeDtypeStruct((rows, feats), BF16),
            ),
            in_specs=[vmem] * 4,
            out_specs=(smem, vmem, vmem),
            compiler_params=pltpu.CompilerParams(vmem_limit_bytes=4 * 1024 * 1024),
        )(*shares)
        return loss[0], grad_q, grad_p

    if mesh is None:
        return shards
    return jax.shard_map(
        shards,
        mesh=mesh,
        in_specs=(P("batch", "mp"), P("batch", "mp"), P("batch"), P()),
        out_specs=(P(), P("batch", "mp"), P("batch", "mp")),
        check_vma=False,
    )


def solution(mesh):
    return build(mesh, GRID)
```

```python
import functools

import jax
import jax.numpy as jnp
from jax import lax
from jax.experimental import pallas as pl
from jax.experimental.pallas import tpu as pltpu
from jax.sharding import PartitionSpec as P

MESH = pl.DeviceIdType.MESH
F32 = jnp.float32
BF16 = jnp.bfloat16
GRID = (2, 8, 8)
NT = (((1,), (1,)), ((), ()))
NN = (((1,), (0,)), ((), ()))
OWN_Q, OWN_P, SWAP_Q, SWAP_P, FAR_Q, FAR_P, CORE, LEFT, RIGHT, ROWS, COLS, GRAD_Q, GRAD_P, OWN_T, SWAP_T, FAR_T,\
    CORE_E, LEFT_E, RIGHT_E, LOSS_Z, LOSS_Y = range(21)


def dot(a, b, dims):
    return lax.dot_general(a, b, dims, preferred_element_type=F32)


def column(row):
    n = row.shape[1]
    return jnp.broadcast_to(row, (n, n)).T


def farthest_first(n):
    return sorted(range(1, n), key=lambda t: -min(t, n - t))


def kernel(grid, scale_any, partner_any, q_any, p_any, rq, rp, loss_z, loss_y,
           scale_ref, partner_ref, q_in, p_in, qb, pb, qn, pn, part, part_core, part_left, part_right,
           first, first_core, first_left, first_right,
           row_stat, row_stats, col_stat, col_stats, gq, gp, tags, q_less, p_less, loss_part, load, send, recv):
    _, gy, gz = grid
    rows, feats = q_in.shape
    half = feats // 2
    nz, ny = gz * rows, gy * rows
    pairs = 2 * gy * nz
    b, m = lax.axis_index("batch"), lax.axis_index("mp")
    x, y, z = b // (gy * gz), b // gz % gy, b % gz

    z_peers = {t: (z + t) % gz for t in farthest_first(gz)}
    y_peers = {t: (y + t) % gy for t in farthest_first(gy)}
    z_peers = [(i, {"batch": (x * gy + y) * gz + i}) for i in z_peers.values()]
    y_peers = [(i, {"batch": (x * gy + i) * gz + z}) for i in y_peers.values()]
    x_peer = {"batch": ((1 - x) * gy + y) * gz + z}
    core, other = m % 2, (m + 2) % 4 // 2 * 2
    core_peer = {"mp": m // 2 * 2 + (m + 1) % 2}
    left_peers = [{"mp": other + c} for c in range(2)]
    right_peers = [{"batch": x_peer["batch"], "mp": other + c} for c in range(2)]

    barrier = pltpu.get_barrier_semaphore()
    everyone = [x_peer] + [d for pair in zip(z_peers, y_peers) for _, d in pair] + [*left_peers, *right_peers, core_peer]
    for d in everyone:
        pl.semaphore_signal(barrier, inc=1, device_id=d, device_id_type=MESH)
    loads = [
        pltpu.make_async_copy(source, target, load.at[i])
        for i, (source, target) in enumerate(
            ((q_any, q_in), (p_any, p_in), (partner_any, partner_ref), (scale_any, scale_ref))
        )
    ]
    for copy in loads:
        copy.start()

    def slot(ref, index, size=16):
        return ref.at[pl.ds(pl.multiple_of(index * size, size), size)]

    sent = []

    def push(src, dst, s, device):
        copy = pltpu.make_async_remote_copy(
            src_ref=src, dst_ref=dst, send_sem=send.at[s], recv_sem=recv.at[s],
            device_id=device, device_id_type=MESH,
        )
        copy.start()

    def arrived(ref, s, count, size):
        view = ref.at[pl.ds(0, count * size)]
        pltpu.make_async_copy(view, view, recv.at[s]).wait()
        sent.append((view, s))

    def departed():
        for view, s in sent:
            pltpu.make_async_copy(view, view, send.at[s]).wait()
        sent.clear()

    def halves(ref):
        whole = ref[...].astype(F32)
        return jnp.concatenate([whole[:, :half], whole[:, half:]], axis=0)

    loads[0].wait()
    slot(qb, z)[...] = halves(q_in).astype(BF16)
    loads[1].wait()
    slot(pb, y)[...] = halves(p_in).astype(BF16)
    pl.semaphore_wait(barrier, len(everyone))

    push(slot(qb, z), slot(qb, gz + z), SWAP_Q, x_peer)
    push(slot(pb, y), slot(pb, gy + y), SWAP_P, x_peer)
    for t in range(max(gy, gz) - 1):
        if t < gz - 1:
            push(slot(qb, z), slot(qb, z), OWN_Q, z_peers[t][1])
        if t < gy - 1:
            push(slot(pb, y), slot(pb, y), OWN_P, y_peers[t][1])

    loads[2].wait()
    loads[3].wait()
    spot = lax.broadcasted_iota(jnp.int32, (1, 1, 2 * nz), 2) % rows
    tag = jnp.zeros((1, 1, 2 * nz), jnp.int32)
    for i in range(rows):
        tag = jnp.where(spot == i, partner_ref[i], tag)
    tags[pl.ds(z, 1)] = tag.astype(F32)
    push(tags.at[pl.ds(z, 1)], tags.at[pl.ds(gz + z, 1)], SWAP_T, x_peer)

    arrived(qb, SWAP_Q, 1, 16)
    for _, device in z_peers[:3]:
        push(slot(qb, gz + z), slot(qb, gz + z), FAR_Q, device)
    arrived(pb, SWAP_P, 1, 16)
    for _, device in y_peers[:3]:
        push(slot(pb, gy + y), slot(pb, gy + y), FAR_P, device)
    for t in range(3, max(gy, gz) - 1):
        if t < gz - 1:
            push(slot(qb, gz + z), slot(qb, gz + z), FAR_Q, z_peers[t][1])
        if t < gy - 1:
            push(slot(pb, gy + y), slot(pb, gy + y), FAR_P, y_peers[t][1])
    arrived(tags, SWAP_T, 1, 1)
    for _, device in z_peers:
        push(tags.at[pl.ds(z, 1)], tags.at[pl.ds(z, 1)], OWN_T, device)
        push(tags.at[pl.ds(gz + z, 1)], tags.at[pl.ds(gz + z, 1)], FAR_T, device)

    def unpack(ref, out, r, n):
        whole = ref[r * n * 16:(r + 1) * n * 16, :half].astype(F32).reshape(n, 2, 8, half)
        whole = jnp.concatenate([whole[:, 0], whole[:, 1]], axis=2).reshape(n * 8, feats)
        out[r * n * 8:(r + 1) * n * 8, :] = whole.astype(BF16)
        square = whole * whole
        width = min(128, feats)
        return sum(square[:, c:c + width] for c in range(0, feats, width))

    arrived(qb, OWN_Q, gz - 1, 16)
    q_near = unpack(qb, qn, 0, gz)
    arrived(pb, OWN_P, gy - 1, 16)
    p_near = unpack(pb, pn, 0, gy)
    nh = nz // 2

    def fold(value):
        return jnp.concatenate([value[:nh], value[nh:]], axis=1)

    def sums(q_square, p_square):
        row = jnp.sum(jnp.concatenate([q_square, p_square], axis=0).T, axis=0, keepdims=True)
        return jnp.broadcast_to(row, (8, 2 * ny))

    first[0:nh, :] = fold(dot(qn[0:nz, :], pn[0:ny, :], NT))
    first[nh:nh + 8, :] = sums(q_near, p_near)
    for device in left_peers:
        push(first, slot(first_left, core, nh + 8), LEFT_E, device)
    for device in right_peers:
        push(first, slot(first_right, core, nh + 8), RIGHT_E, device)
    push(first, first_core, CORE_E, core_peer)

    arrived(pb, FAR_P, gy - 1, 16)
    p_far = unpack(pb, pn, 1, gy)
    part[nz:nz + nh, :] = fold(dot(qn[0:nz, :], pn[ny:, :], NT))
    for device in left_peers:
        push(part.at[pl.ds(nz, nh)], slot(part_left, core, nh), LEFT, device)
    for device in right_peers:
        push(part.at[pl.ds(nz, nh)], slot(part_right, core, nh), RIGHT, device)
    arrived(qb, FAR_Q, gz - 1, 16)
    q_far = unpack(qb, qn, 1, gz)

    part[0:nz, :] = dot(qn[nz:, :], pn[...], NT)
    part[nz + nh:nz + nh + 8, :] = sums(q_far, p_far)
    push(part, part_core, CORE, core_peer)
    arrived(tags, OWN_T, gz - 1, 1)
    arrived(tags, FAR_T, gz - 1, 1)
    seat = lax.broadcasted_iota(jnp.int32, (2 * gz, 1, 2 * nz), 2) // rows
    taken = seat == lax.broadcasted_iota(jnp.int32, (2 * gz, 1, 2 * nz), 0)
    partner = column(jnp.sum(jnp.where(taken, tags[...], 0.0), axis=0))
    lane = lax.broadcasted_iota(jnp.int32, (1, 2 * ny), 1)
    columns = (((x + lane // ny) % 2 * gy + lane // rows % gy) * gz + z) * rows + lane % rows
    hit = partner == columns.astype(F32)
    arrived(first_core, CORE_E, 1, nh + 8)
    arrived(first_left, LEFT_E, 2, nh + 8)
    arrived(first_right, RIGHT_E, 2, nh + 8)
    near = (first[...] + first_core[...]) + (first_left[0:nh + 8, :] + first_left[nh + 8:, :])
    right_near = first_right[0:nh + 8, :] + first_right[nh + 8:, :]
    arrived(part_core, CORE, 1, 3 * nh + 8)
    total = part[...] + part_core[...]
    arrived(part_left, LEFT, 2, nh)
    left = total[nz:nz + nh] + (part_left[0:nh, :] + part_left[nh:, :])
    arrived(part_right, RIGHT, 2, nh)
    right = part_right[0:nh, :] + part_right[nh:, :]
    lower = lane < ny

    def beside(a, b):
        return jnp.concatenate(
            [jnp.where(lower, a, pltpu.roll(b, ny, 1)), jnp.where(lower, pltpu.roll(a, ny, 1), b)], axis=0
        )

    product = jnp.concatenate([beside(near[:nh], left), total[:nz] + beside(right, right_near[:nh])], axis=0)
    squares = beside(near[nh:nh + 8], total[nz + nh:] + right_near[nh:])

    scale = scale_ref[0]
    q_inv = column(lax.rsqrt(squares[0:1] + 1e-6))
    p_inv = lax.rsqrt(squares[8:9] + 1e-6)
    scores = (product * q_inv) * p_inv * scale
    across = scores.T

    def added(value, n):
        return jnp.sum(value[:n], axis=0, keepdims=True) + jnp.sum(value[n:], axis=0, keepdims=True)

    def both(row, n):
        return jnp.sum(row[:, :n]) + jnp.sum(row[:, n:])

    row_max = jnp.max(across, axis=0, keepdims=True)
    row_exp = jnp.exp(across - row_max)
    row_sum = added(row_exp, ny)
    col_max = jnp.max(scores, axis=0, keepdims=True)
    col_exp = jnp.exp(scores - col_max)
    col_sum = added(col_exp, nz)
    held = jnp.where(hit, scores, 0.0)
    near, far = (jnp.sum(held[r:r + nz], axis=0, keepdims=True) for r in (0, nz))
    hits = (jnp.sum(near[:, :ny]) + jnp.sum(far[:, ny:])) + (jnp.sum(near[:, ny:]) + jnp.sum(far[:, :ny]))
    for i, value in enumerate((row_max, row_sum, jnp.full((1, 2 * nz), hits))):
        row_stat[i] = value
    for i, value in enumerate((col_max, col_sum)):
        col_stat[i] = value
    for t in range(max(gy, gz) - 1):
        if t < gz - 1:
            push(row_stat, slot(row_stats, z, 3), ROWS, z_peers[t][1])
        if t < gy - 1:
            push(col_stat, slot(col_stats, y, 2), COLS, y_peers[t][1])
    slot(row_stats, z, 3)[...] = row_stat[...]
    slot(col_stats, y, 2)[...] = col_stat[...]

    def units(raw, inv, less, n):
        inv = inv[:, :1]
        unit = raw[...].astype(F32) * inv
        raw[...] = unit.astype(BF16)
        less[...] = unit[:n] * inv[:n]
        return scale * inv[:n]

    q_scale = units(qn, q_inv, q_less, nz)
    p_scale = units(pn, column(p_inv), p_less, ny)
    row_exp = row_exp.T * (0.5 / pairs)
    col_exp = col_exp * (0.5 / pairs)
    hit = jnp.where(hit, 1.0 / pairs, 0.0)

    def lse(ref, n):
        stats = ref[...].reshape(n, -1, 1, ref.shape[2])
        most = jnp.max(stats[:, 0], axis=0)
        summed = jnp.sum(stats[:, 1] * jnp.exp(stats[:, 0] - most), axis=0)
        return most + jnp.log(summed), stats

    arrived(row_stats, ROWS, gz - 1, 3)
    row_lse, stats = lse(row_stats, gz)
    row_part = column(jnp.exp(row_max - row_lse))
    arrived(col_stats, COLS, gy - 1, 2)
    col_lse, _ = lse(col_stats, gy)

    weights = row_exp * row_part + col_exp * jnp.exp(col_max - col_lse) - hit
    weights = weights.astype(BF16).astype(F32)
    turned = weights.T[:ny]
    weights = weights[:nz]

    def share(weight, score, other, scaled, less):
        n = weight.shape[0]
        d = dot(weight.astype(BF16), other, NN)
        along = jnp.sum(weight * score, axis=1, keepdims=True)
        d = (d * scaled - less * along).reshape(n // 8, 8, feats)
        return jnp.concatenate([d[:, :, :half], d[:, :, half:]], axis=1).reshape(n * 2, half)

    positives = jnp.sum(stats[:, 2, 0, 0:1])
    loss_part[0] = jnp.full((1, 128), 0.5 * both(col_lse, ny))
    loss_part[1] = jnp.full((1, 128), 0.5 * both(row_lse, nz) - positives)
    for _, device in z_peers:
        push(loss_part.at[pl.ds(0, 1)], loss_z.at[pl.ds(z, 1)], LOSS_Z, device)
    for _, device in y_peers:
        push(loss_part.at[pl.ds(1, 1)], loss_y.at[pl.ds(y, 1)], LOSS_Y, device)

    gq[...] = share(weights, scores[:nz], pn[...], q_scale, q_less[...]).astype(BF16)
    for i, device in z_peers[:3]:
        push(slot(gq, i), slot(rq, z), GRAD_Q, device)
    gp[...] = share(turned, across[:ny], qn[...], p_scale, p_less[...]).astype(BF16)
    for i, device in y_peers[:3]:
        push(slot(gp, i), slot(rp, y), GRAD_P, device)
    for t in range(3, max(gy, gz) - 1):
        if t < gz - 1:
            push(slot(gq, z_peers[t][0]), slot(rq, z), GRAD_Q, z_peers[t][1])
        if t < gy - 1:
            push(slot(gp, y_peers[t][0]), slot(rp, y), GRAD_P, y_peers[t][1])
    keeps = [
        pltpu.make_async_copy(source, target, load.at[i])
        for i, (source, target) in enumerate((
            (slot(gq, z), slot(rq, z)),
            (slot(gp, y), slot(rp, y)),
            (loss_part.at[pl.ds(0, 1)], loss_z.at[pl.ds(z, 1)]),
            (loss_part.at[pl.ds(1, 1)], loss_y.at[pl.ds(y, 1)]),
        ))
    ]
    for copy in keeps:
        copy.start()
    for copy in keeps:
        copy.wait()
    departed()
    arrived(rq, GRAD_Q, gz - 1, 16)
    arrived(rp, GRAD_P, gy - 1, 16)
    arrived(loss_z, LOSS_Z, gz - 1, 1)
    arrived(loss_y, LOSS_Y, gy - 1, 1)
    departed()


def finish(pairs, rq, rp, loss_z, loss_y, loss_ref, gq_ref, gp_ref):
    half = gq_ref.shape[1] // 2

    for ref, out_ref in ((rq, gq_ref), (rp, gp_ref)):
        whole = jnp.sum(ref[...].astype(F32).reshape(-1, 16, half), axis=0)
        out_ref[...] = jnp.concatenate([whole[:8], whole[8:]], axis=1).astype(BF16)
    parts = jnp.sum(loss_z[...], axis=0) + jnp.sum(loss_y[...], axis=0)
    loss_ref[0] = jnp.sum(parts[:, 0:1]) / pairs


def build(mesh, grid):
    _, gy, gz = grid

    def shards(queries, paraphrases, partner, logit_scale):
        rows, feats = queries.shape
        half = feats // 2
        nz, ny = gz * rows, gy * rows
        vmem, smem = pl.BlockSpec(memory_space=pltpu.VMEM), pl.BlockSpec(memory_space=pltpu.SMEM)
        anywhere = pl.BlockSpec(memory_space=pl.ANY)
        block = pltpu.VMEM((nz + nz // 2 + 8, 2 * ny), F32)
        shares = pl.pallas_call(
            functools.partial(kernel, grid),
            out_shape=(
                jax.ShapeDtypeStruct((gz * 16, half), BF16),
                jax.ShapeDtypeStruct((gy * 16, half), BF16),
                jax.ShapeDtypeStruct((gz, 1, 128), F32),
                jax.ShapeDtypeStruct((gy, 1, 128), F32),
            ),
            in_specs=[anywhere] * 4,
            out_specs=(anywhere,) * 4,
            scratch_shapes=[
                pltpu.SMEM((1,), F32),
                pltpu.SMEM((rows,), jnp.int32),
                pltpu.VMEM((rows, feats), BF16),
                pltpu.VMEM((rows, feats), BF16),
                pltpu.VMEM((gz * 32, half), BF16),
                pltpu.VMEM((gy * 32, half), BF16),
                pltpu.VMEM((2 * nz, feats), BF16),
                pltpu.VMEM((2 * ny, feats), BF16),
                block,
                block,
                pltpu.VMEM((nz, 2 * ny), F32),
                pltpu.VMEM((nz, 2 * ny), F32),
                pltpu.VMEM((nz // 2 + 8, 2 * ny), F32),
                pltpu.VMEM((nz // 2 + 8, 2 * ny), F32),
                pltpu.VMEM((nz + 16, 2 * ny), F32),
                pltpu.VMEM((nz + 16, 2 * ny), F32),
                pltpu.VMEM((3, 1, 2 * nz), F32),
                pltpu.VMEM((gz * 3, 1, 2 * nz), F32),
                pltpu.VMEM((2, 1, 2 * ny), F32),
                pltpu.VMEM((gy * 2, 1, 2 * ny), F32),
                pltpu.VMEM((gz * 16, half), BF16),
                pltpu.VMEM((gy * 16, half), BF16),
                pltpu.VMEM((2 * gz, 1, 2 * nz), F32),
                pltpu.VMEM((nz, feats), F32),
                pltpu.VMEM((ny, feats), F32),
                pltpu.VMEM((2, 1, 128), F32),
                pltpu.SemaphoreType.DMA((4,)),
                pltpu.SemaphoreType.DMA((21,)),
                pltpu.SemaphoreType.DMA((21,)),
            ],
            compiler_params=pltpu.CompilerParams(
                collective_id=0, has_side_effects=True, vmem_limit_bytes=32 * 1024 * 1024
            ),
        )(logit_scale.reshape(1), pltpu.with_memory_space_constraint(partner, pltpu.HBM), pltpu.with_memory_space_constraint(queries, pltpu.HBM), pltpu.with_memory_space_constraint(paraphrases, pltpu.HBM))
        loss, grad_q, grad_p = pl.pallas_call(
            functools.partial(finish, 2 * gy * nz),
            out_shape=(
                jax.ShapeDtypeStruct((1,), F32),
                jax.ShapeDtypeStruct((rows, feats), BF16),
                jax.ShapeDtypeStruct((rows, feats), BF16),
            ),
            in_specs=[vmem] * 4,
            out_specs=(smem, vmem, vmem),
            compiler_params=pltpu.CompilerParams(vmem_limit_bytes=4 * 1024 * 1024),
        )(*shares)
        return loss[0], grad_q, grad_p

    if mesh is None:
        return shards
    return jax.shard_map(
        shards,
        mesh=mesh,
        in_specs=(P("batch", "mp"), P("batch", "mp"), P("batch"), P()),
        out_specs=(P(), P("batch", "mp"), P("batch", "mp")),
        check_vma=False,
    )


def solution(mesh):
    return build(mesh, GRID)
```

```python
import functools

import jax
import jax.numpy as jnp
from jax import lax
from jax.experimental import pallas as pl
from jax.experimental.pallas import tpu as pltpu
from jax.sharding import PartitionSpec as P

MESH = pl.DeviceIdType.MESH
F32 = jnp.float32
BF16 = jnp.bfloat16
GRID = (2, 8, 8)
NT = (((1,), (1,)), ((), ()))
NN = (((1,), (0,)), ((), ()))
OWN_Q, OWN_P, SWAP_Q, SWAP_P, FAR_Q, FAR_P, CORE, LEFT, RIGHT, ROWS, COLS, GRAD_Q, GRAD_P, OWN_T, SWAP_T, FAR_T,\
    CORE_E, LEFT_E, RIGHT_E, LOSS_Z, LOSS_Y = range(21)


def dot(a, b, dims):
    return lax.dot_general(a, b, dims, preferred_element_type=F32)


def column(row):
    n = row.shape[1]
    return jnp.broadcast_to(row, (n, n)).T


def farthest_first(n):
    return sorted(range(1, n), key=lambda t: -min(t, n - t))


def kernel(grid, scale_ref, partner_any, q_any, p_any, rq, rp, loss_z, loss_y,
           partner_ref, q_in, p_in, qb, pb, qn, pn, part, part_core, part_left, part_right,
           first, first_core, first_left, first_right,
           row_stat, row_stats, col_stat, col_stats, gq, gp, tags, q_less, p_less, loss_part, load, send, recv):
    _, gy, gz = grid
    rows, feats = q_in.shape
    half = feats // 2
    nz, ny = gz * rows, gy * rows
    pairs = 2 * gy * nz
    b, m = lax.axis_index("batch"), lax.axis_index("mp")
    x, y, z = b // (gy * gz), b // gz % gy, b % gz

    z_peers = {t: (z + t) % gz for t in farthest_first(gz)}
    y_peers = {t: (y + t) % gy for t in farthest_first(gy)}
    z_peers = [(i, {"batch": (x * gy + y) * gz + i}) for i in z_peers.values()]
    y_peers = [(i, {"batch": (x * gy + i) * gz + z}) for i in y_peers.values()]
    x_peer = {"batch": ((1 - x) * gy + y) * gz + z}
    core, other = m % 2, (m + 2) % 4 // 2 * 2
    core_peer = {"mp": m // 2 * 2 + (m + 1) % 2}
    left_peers = [{"mp": other + c} for c in range(2)]
    right_peers = [{"batch": x_peer["batch"], "mp": other + c} for c in range(2)]

    barrier = pltpu.get_barrier_semaphore()
    everyone = [x_peer] + [d for pair in zip(z_peers, y_peers) for _, d in pair] + [*left_peers, *right_peers, core_peer]
    for d in everyone:
        pl.semaphore_signal(barrier, inc=1, device_id=d, device_id_type=MESH)
    loads = [
        pltpu.make_async_copy(source, target, load.at[i])
        for i, (source, target) in enumerate(
            ((q_any, q_in), (p_any, p_in), (partner_any, partner_ref))
        )
    ]
    for copy in loads:
        copy.start()

    def slot(ref, index, size=16):
        return ref.at[pl.ds(pl.multiple_of(index * size, size), size)]

    sent = []

    def push(src, dst, s, device):
        copy = pltpu.make_async_remote_copy(
            src_ref=src, dst_ref=dst, send_sem=send.at[s], recv_sem=recv.at[s],
            device_id=device, device_id_type=MESH,
        )
        copy.start()

    def arrived(ref, s, count, size):
        view = ref.at[pl.ds(0, count * size)]
        pltpu.make_async_copy(view, view, recv.at[s]).wait()
        sent.append((view, s))

    def departed():
        for view, s in sent:
            pltpu.make_async_copy(view, view, send.at[s]).wait()
        sent.clear()

    def halves(ref):
        whole = ref[...].astype(F32)
        return jnp.concatenate([whole[:, :half], whole[:, half:]], axis=0)

    loads[0].wait()
    slot(qb, z)[...] = halves(q_in).astype(BF16)
    loads[1].wait()
    slot(pb, y)[...] = halves(p_in).astype(BF16)
    pl.semaphore_wait(barrier, len(everyone))

    push(slot(qb, z), slot(qb, gz + z), SWAP_Q, x_peer)
    push(slot(pb, y), slot(pb, gy + y), SWAP_P, x_peer)
    for t in range(max(gy, gz) - 1):
        if t < gz - 1:
            push(slot(qb, z), slot(qb, z), OWN_Q, z_peers[t][1])
        if t < gy - 1:
            push(slot(pb, y), slot(pb, y), OWN_P, y_peers[t][1])

    loads[2].wait()
    spot = lax.broadcasted_iota(jnp.int32, (1, 1, 2 * nz), 2) % rows
    tag = jnp.zeros((1, 1, 2 * nz), jnp.int32)
    for i in range(rows):
        tag = jnp.where(spot == i, partner_ref[i], tag)
    tags[pl.ds(z, 1)] = tag.astype(F32)
    push(tags.at[pl.ds(z, 1)], tags.at[pl.ds(gz + z, 1)], SWAP_T, x_peer)

    arrived(qb, SWAP_Q, 1, 16)
    for _, device in z_peers[:3]:
        push(slot(qb, gz + z), slot(qb, gz + z), FAR_Q, device)
    arrived(pb, SWAP_P, 1, 16)
    for _, device in y_peers[:3]:
        push(slot(pb, gy + y), slot(pb, gy + y), FAR_P, device)
    for t in range(3, max(gy, gz) - 1):
        if t < gz - 1:
            push(slot(qb, gz + z), slot(qb, gz + z), FAR_Q, z_peers[t][1])
        if t < gy - 1:
            push(slot(pb, gy + y), slot(pb, gy + y), FAR_P, y_peers[t][1])
    arrived(tags, SWAP_T, 1, 1)
    for _, device in z_peers:
        push(tags.at[pl.ds(z, 1)], tags.at[pl.ds(z, 1)], OWN_T, device)
        push(tags.at[pl.ds(gz + z, 1)], tags.at[pl.ds(gz + z, 1)], FAR_T, device)

    def unpack(ref, out, r, n):
        whole = ref[r * n * 16:(r + 1) * n * 16, :half].astype(F32).reshape(n, 2, 8, half)
        whole = jnp.concatenate([whole[:, 0], whole[:, 1]], axis=2).reshape(n * 8, feats)
        out[r * n * 8:(r + 1) * n * 8, :] = whole.astype(BF16)
        square = whole * whole
        width = min(128, feats)
        return sum(square[:, c:c + width] for c in range(0, feats, width))

    arrived(qb, OWN_Q, gz - 1, 16)
    q_near = unpack(qb, qn, 0, gz)
    arrived(pb, OWN_P, gy - 1, 16)
    p_near = unpack(pb, pn, 0, gy)
    nh = nz // 2

    def fold(value):
        return jnp.concatenate([value[:nh], value[nh:]], axis=1)

    def sums(q_square, p_square):
        row = jnp.sum(jnp.concatenate([q_square, p_square], axis=0).T, axis=0, keepdims=True)
        return jnp.broadcast_to(row, (8, 2 * ny))

    first[0:nh, :] = fold(dot(qn[0:nz, :], pn[0:ny, :], NT))
    first[nh:nh + 8, :] = sums(q_near, p_near)
    for device in left_peers:
        push(first, slot(first_left, core, nh + 8), LEFT_E, device)
    for device in right_peers:
        push(first, slot(first_right, core, nh + 8), RIGHT_E, device)
    push(first, first_core, CORE_E, core_peer)

    arrived(pb, FAR_P, gy - 1, 16)
    p_far = unpack(pb, pn, 1, gy)
    part[nz:nz + nh, :] = fold(dot(qn[0:nz, :], pn[ny:, :], NT))
    for device in left_peers:
        push(part.at[pl.ds(nz, nh)], slot(part_left, core, nh), LEFT, device)
    for device in right_peers:
        push(part.at[pl.ds(nz, nh)], slot(part_right, core, nh), RIGHT, device)
    arrived(qb, FAR_Q, gz - 1, 16)
    q_far = unpack(qb, qn, 1, gz)

    part[0:nz, :] = dot(qn[nz:, :], pn[...], NT)
    part[nz + nh:nz + nh + 8, :] = sums(q_far, p_far)
    push(part, part_core, CORE, core_peer)
    arrived(tags, OWN_T, gz - 1, 1)
    arrived(tags, FAR_T, gz - 1, 1)
    seat = lax.broadcasted_iota(jnp.int32, (2 * gz, 1, 2 * nz), 2) // rows
    taken = seat == lax.broadcasted_iota(jnp.int32, (2 * gz, 1, 2 * nz), 0)
    partner = column(jnp.sum(jnp.where(taken, tags[...], 0.0), axis=0))
    lane = lax.broadcasted_iota(jnp.int32, (1, 2 * ny), 1)
    columns = (((x + lane // ny) % 2 * gy + lane // rows % gy) * gz + z) * rows + lane % rows
    hit = partner == columns.astype(F32)
    arrived(first_core, CORE_E, 1, nh + 8)
    arrived(first_left, LEFT_E, 2, nh + 8)
    arrived(first_right, RIGHT_E, 2, nh + 8)
    near = (first[...] + first_core[...]) + (first_left[0:nh + 8, :] + first_left[nh + 8:, :])
    right_near = first_right[0:nh + 8, :] + first_right[nh + 8:, :]
    arrived(part_core, CORE, 1, 3 * nh + 8)
    total = part[...] + part_core[...]
    arrived(part_left, LEFT, 2, nh)
    left = total[nz:nz + nh] + (part_left[0:nh, :] + part_left[nh:, :])
    arrived(part_right, RIGHT, 2, nh)
    right = part_right[0:nh, :] + part_right[nh:, :]
    lower = lane < ny

    def beside(a, b):
        return jnp.concatenate(
            [jnp.where(lower, a, pltpu.roll(b, ny, 1)), jnp.where(lower, pltpu.roll(a, ny, 1), b)], axis=0
        )

    product = jnp.concatenate([beside(near[:nh], left), total[:nz] + beside(right, right_near[:nh])], axis=0)
    squares = beside(near[nh:nh + 8], total[nz + nh:] + right_near[nh:])

    scale = scale_ref[...]
    q_inv = column(lax.rsqrt(squares[0:1] + 1e-6))
    p_inv = lax.rsqrt(squares[8:9] + 1e-6)
    scores = (product * q_inv) * p_inv * scale
    across = scores.T

    def added(value, n):
        return jnp.sum(value[:n], axis=0, keepdims=True) + jnp.sum(value[n:], axis=0, keepdims=True)

    def both(row, n):
        return jnp.sum(row[:, :n]) + jnp.sum(row[:, n:])

    row_max = jnp.max(across, axis=0, keepdims=True)
    row_exp = jnp.exp(across - row_max)
    row_sum = added(row_exp, ny)
    col_max = jnp.max(scores, axis=0, keepdims=True)
    col_exp = jnp.exp(scores - col_max)
    col_sum = added(col_exp, nz)
    held = jnp.where(hit, scores, 0.0)
    near, far = (jnp.sum(held[r:r + nz], axis=0, keepdims=True) for r in (0, nz))
    hits = (jnp.sum(near[:, :ny]) + jnp.sum(far[:, ny:])) + (jnp.sum(near[:, ny:]) + jnp.sum(far[:, :ny]))
    for i, value in enumerate((row_max, row_sum, jnp.full((1, 2 * nz), hits))):
        row_stat[i] = value
    for i, value in enumerate((col_max, col_sum)):
        col_stat[i] = value
    for t in range(max(gy, gz) - 1):
        if t < gz - 1:
            push(row_stat, slot(row_stats, z, 3), ROWS, z_peers[t][1])
        if t < gy - 1:
            push(col_stat, slot(col_stats, y, 2), COLS, y_peers[t][1])
    slot(row_stats, z, 3)[...] = row_stat[...]
    slot(col_stats, y, 2)[...] = col_stat[...]

    def units(raw, inv, less, n):
        inv = inv[:, :1]
        unit = raw[...].astype(F32) * inv
        raw[...] = unit.astype(BF16)
        less[...] = unit[:n] * inv[:n]
        return scale * inv[:n]

    q_scale = units(qn, q_inv, q_less, nz)
    p_scale = units(pn, column(p_inv), p_less, ny)
    row_exp = row_exp.T * (0.5 / pairs)
    col_exp = col_exp * (0.5 / pairs)
    hit = jnp.where(hit, 1.0 / pairs, 0.0)

    def lse(ref, n):
        stats = ref[...].reshape(n, -1, 1, ref.shape[2])
        most = jnp.max(stats[:, 0], axis=0)
        summed = jnp.sum(stats[:, 1] * jnp.exp(stats[:, 0] - most), axis=0)
        return most + jnp.log(summed), stats

    arrived(row_stats, ROWS, gz - 1, 3)
    row_lse, stats = lse(row_stats, gz)
    row_part = column(jnp.exp(row_max - row_lse))
    arrived(col_stats, COLS, gy - 1, 2)
    col_lse, _ = lse(col_stats, gy)

    weights = row_exp * row_part + col_exp * jnp.exp(col_max - col_lse) - hit
    weights = weights.astype(BF16).astype(F32)
    turned = weights.T[:ny]
    weights = weights[:nz]

    def share(weight, score, other, scaled, less):
        n = weight.shape[0]
        d = dot(weight.astype(BF16), other, NN)
        along = jnp.sum(weight * score, axis=1, keepdims=True)
        d = (d * scaled - less * along).reshape(n // 8, 8, feats)
        return jnp.concatenate([d[:, :, :half], d[:, :, half:]], axis=1).reshape(n * 2, half)

    positives = jnp.sum(stats[:, 2, 0, 0:1])
    loss_part[0] = jnp.full((1, 128), 0.5 * both(col_lse, ny))
    loss_part[1] = jnp.full((1, 128), 0.5 * both(row_lse, nz) - positives)
    for _, device in z_peers:
        push(loss_part.at[pl.ds(0, 1)], loss_z.at[pl.ds(z, 1)], LOSS_Z, device)
    for _, device in y_peers:
        push(loss_part.at[pl.ds(1, 1)], loss_y.at[pl.ds(y, 1)], LOSS_Y, device)

    gq[...] = share(weights, scores[:nz], pn[...], q_scale, q_less[...]).astype(BF16)
    for i, device in z_peers[:3]:
        push(slot(gq, i), slot(rq, z), GRAD_Q, device)
    gp[...] = share(turned, across[:ny], qn[...], p_scale, p_less[...]).astype(BF16)
    for i, device in y_peers[:3]:
        push(slot(gp, i), slot(rp, y), GRAD_P, device)
    for t in range(3, max(gy, gz) - 1):
        if t < gz - 1:
            push(slot(gq, z_peers[t][0]), slot(rq, z), GRAD_Q, z_peers[t][1])
        if t < gy - 1:
            push(slot(gp, y_peers[t][0]), slot(rp, y), GRAD_P, y_peers[t][1])
    keeps = [
        pltpu.make_async_copy(source, target, load.at[i])
        for i, (source, target) in enumerate((
            (slot(gq, z), slot(rq, z)),
            (slot(gp, y), slot(rp, y)),
            (loss_part.at[pl.ds(0, 1)], loss_z.at[pl.ds(z, 1)]),
            (loss_part.at[pl.ds(1, 1)], loss_y.at[pl.ds(y, 1)]),
        ))
    ]
    for copy in keeps:
        copy.start()
    for copy in keeps:
        copy.wait()
    departed()
    arrived(rq, GRAD_Q, gz - 1, 16)
    arrived(rp, GRAD_P, gy - 1, 16)
    arrived(loss_z, LOSS_Z, gz - 1, 1)
    arrived(loss_y, LOSS_Y, gy - 1, 1)
    departed()


def finish(pairs, rq, rp, loss_z, loss_y, loss_ref, gq_ref, gp_ref):
    half = gq_ref.shape[1] // 2

    for ref, out_ref in ((rq, gq_ref), (rp, gp_ref)):
        whole = jnp.sum(ref[...].astype(F32).reshape(-1, 16, half), axis=0)
        out_ref[...] = jnp.concatenate([whole[:8], whole[8:]], axis=1).astype(BF16)
    parts = jnp.sum(loss_z[...], axis=0) + jnp.sum(loss_y[...], axis=0)
    loss_ref[0] = jnp.sum(parts[:, 0:1]) / pairs


def build(mesh, grid):
    _, gy, gz = grid

    def shards(queries, paraphrases, partner, logit_scale):
        rows, feats = queries.shape
        half = feats // 2
        nz, ny = gz * rows, gy * rows
        vmem, smem = pl.BlockSpec(memory_space=pltpu.VMEM), pl.BlockSpec(memory_space=pltpu.SMEM)
        anywhere = pl.BlockSpec(memory_space=pl.ANY)
        block = pltpu.VMEM((nz + nz // 2 + 8, 2 * ny), F32)
        shares = pl.pallas_call(
            functools.partial(kernel, grid),
            out_shape=(
                jax.ShapeDtypeStruct((gz * 16, half), BF16),
                jax.ShapeDtypeStruct((gy * 16, half), BF16),
                jax.ShapeDtypeStruct((gz, 1, 128), F32),
                jax.ShapeDtypeStruct((gy, 1, 128), F32),
            ),
            grid_spec=pltpu.PrefetchScalarGridSpec(num_scalar_prefetch=1, grid=(), in_specs=[anywhere] * 3, out_specs=(anywhere,) * 4, scratch_shapes=[
                pltpu.SMEM((rows,), jnp.int32),
                pltpu.VMEM((rows, feats), BF16),
                pltpu.VMEM((rows, feats), BF16),
                pltpu.VMEM((gz * 32, half), BF16),
                pltpu.VMEM((gy * 32, half), BF16),
                pltpu.VMEM((2 * nz, feats), BF16),
                pltpu.VMEM((2 * ny, feats), BF16),
                block,
                block,
                pltpu.VMEM((nz, 2 * ny), F32),
                pltpu.VMEM((nz, 2 * ny), F32),
                pltpu.VMEM((nz // 2 + 8, 2 * ny), F32),
                pltpu.VMEM((nz // 2 + 8, 2 * ny), F32),
                pltpu.VMEM((nz + 16, 2 * ny), F32),
                pltpu.VMEM((nz + 16, 2 * ny), F32),
                pltpu.VMEM((3, 1, 2 * nz), F32),
                pltpu.VMEM((gz * 3, 1, 2 * nz), F32),
                pltpu.VMEM((2, 1, 2 * ny), F32),
                pltpu.VMEM((gy * 2, 1, 2 * ny), F32),
                pltpu.VMEM((gz * 16, half), BF16),
                pltpu.VMEM((gy * 16, half), BF16),
                pltpu.VMEM((2 * gz, 1, 2 * nz), F32),
                pltpu.VMEM((nz, feats), F32),
                pltpu.VMEM((ny, feats), F32),
                pltpu.VMEM((2, 1, 128), F32),
                pltpu.SemaphoreType.DMA((4,)),
                pltpu.SemaphoreType.DMA((21,)),
                pltpu.SemaphoreType.DMA((21,)),
            ]),
            compiler_params=pltpu.CompilerParams(
                collective_id=0, has_side_effects=True, vmem_limit_bytes=32 * 1024 * 1024
            ),
        )(logit_scale, pltpu.with_memory_space_constraint(partner, pltpu.HBM), pltpu.with_memory_space_constraint(queries, pltpu.HBM), pltpu.with_memory_space_constraint(paraphrases, pltpu.HBM))
        loss, grad_q, grad_p = pl.pallas_call(
            functools.partial(finish, 2 * gy * nz),
            out_shape=(
                jax.ShapeDtypeStruct((1,), F32),
                jax.ShapeDtypeStruct((rows, feats), BF16),
                jax.ShapeDtypeStruct((rows, feats), BF16),
            ),
            in_specs=[vmem] * 4,
            out_specs=(smem, vmem, vmem),
            compiler_params=pltpu.CompilerParams(vmem_limit_bytes=4 * 1024 * 1024),
        )(*shares)
        return loss[0], grad_q, grad_p

    if mesh is None:
        return shards
    return jax.shard_map(
        shards,
        mesh=mesh,
        in_specs=(P("batch", "mp"), P("batch", "mp"), P("batch"), P()),
        out_specs=(P(), P("batch", "mp"), P("batch", "mp")),
        check_vma=False,
    )


def solution(mesh):
    return build(mesh, GRID)
```
